512 devices in a mesh: expert: 16 (over x, z_hi, core), shard: 8 (over y), replica: 4 (over z_lo).
Axes of the slice: x: 4, y: 8, z: 8 (z_hi: 2, z_lo: 4; z = z_hi * 4 + z_lo), core: 2. Of those that a mesh axis runs over, the one named last changes fastest.
Arguments:
- grad_out: bfloat16 [1024, 3072], P('expert'), may hold values from -6 to 6
- gate_probs: bfloat16 [1024, 4], P('expert'), may hold values from 0.049804688 to 1
- expert_ids: int32 [1024, 4], P('expert'), may hold values from 0 to 15, all different within a row; in each aligned block of 64 rows (0 to 63, 64 to 127, ...) at most 32 rows name the same one
- saved_hidden: bfloat16 [16, 5376, 512], P('expert', ('shard', 'replica')), may hold values from -6 to 6
- down_weight: bfloat16 [16, 5376, 3072], P('expert', ('shard', 'replica')), may hold values from -0.078125 to 0.078125
Outputs:
- grad_hidden: bfloat16 [16, 5376, 512], P('expert', ('shard', 'replica'))
- grad_down: bfloat16 [16, 5376, 3072], P('expert', ('shard', 'replica'))
- grad_gates: float32 [1024, 4], P('expert')
The draws below stay inside these ranges and needn't reach their ends.
Inputs may be any that keep to these rules, and one draw needn't show every extreme that they name: `expert_ids`: each row names 4 different experts. In each aligned block of 64 rows, no expert is named by more than 32 rows, a bound that some block reaches.
All inputs are finite; a program needn't handle non-finite values.
Results may differ from the reference program's by a relative error of at most 0.0049.
Values may be sent and summed in bfloat16 or wider, within the bound.
A program may use at most 64 MiB of HBM per device.

```python
import math
import jax
import jax.numpy as jnp
import numpy as np
from jax import lax

D = 3072
FF = 5376
TOP = 4
TOK_DEV = 64
EXPERTS = 16
CAP = 32
ROWS = 512
TOKENS = 1024
N_EXPERT = 16


def block_scale(own_key, shape, cuts, smallest, top_value):
    gain = 1.0
    for axis_at, shards_of in cuts:
        heights = jax.random.uniform(jax.random.fold_in(jax.random.fold_in(own_key, 6), axis_at), (shards_of,), jnp.float32, smallest / len(cuts), top_value / len(cuts))
        gain = gain * jnp.repeat(jnp.exp(heights), shape[axis_at] // shards_of).reshape((-1,) + (1,) * (len(shape) - 1 - axis_at))
    return gain


def deal_out(own_key, own, number, rows, amount, top, bound, skew):
    ranking = jax.random.permutation(own_key, amount)
    crowded, usual = load_shares(amount, rows * top, bound, skew, True), load_shares(amount, rows * top, bound, skew, False)
    places = jnp.arange(amount)

    def named(tallies, offset_by):
        used = int((tallies > 0).sum())
        fixed = max(1, used // 4)
        shifted = fixed + (places - fixed + offset_by * (used - fixed)) % max(1, amount - fixed)
        return jnp.zeros((amount,), jnp.int32).at[ranking[jnp.where(places < fixed, places, shifted)]].set(jnp.asarray(tallies, jnp.int32))

    tallies = jnp.where(number % 4 == 0, named(crowded, number // 4), named(usual, number - number // 4 - 1))
    mixed = jax.random.permutation(jax.random.fold_in(own, 3), amount)
    giver, taker = mixed[0:amount // 2 * 2:2], mixed[1:amount // 2 * 2:2]
    room = jnp.minimum(tallies[giver] - 1, bound - tallies[taker]) // 2
    room = jnp.where((giver == ranking[0]) | (taker == ranking[0]) | (tallies[taker] == 0), 0, jnp.maximum(room, 0))
    shifted = jax.random.randint(jax.random.fold_in(own, 4), (amount // 2,), 0, 1 << 20) % (room + 1)
    tallies = tallies.at[giver].add(-shifted).at[taker].add(shifted)
    labels = jnp.searchsorted(jnp.cumsum(tallies), jnp.arange(rows * top), side="right").astype(jnp.int32)
    listing = labels.reshape(top, rows).T
    listing = listing[jax.random.permutation(jax.random.fold_in(own, 1), rows)]
    offset_by = jax.random.randint(jax.random.fold_in(own, 2), (rows, 1), 0, top)
    return jnp.take_along_axis(listing, (jnp.arange(top)[None, :] + offset_by) % top, axis=1)


def load_shares(amount, total, limit, slope, full):
    loads = [(1 << 20) // math.isqrt(grade ** slope) + 1 for grade in range(1, amount + 1)]
    largest = limit if full else min(limit, max(-(-total // amount), total * loads[0] // sum(loads)))
    least = 1 if total - largest >= amount - 1 else 0
    counts, spare = [largest] + [least] * (amount - 1), total - largest - least * (amount - 1)
    while spare > 0:
        free = [i for i in range(1, amount) if counts[i] < largest] or [i for i in range(1, amount) if counts[i] < limit]
        whole, budget = sum([loads[i] for i in free]), spare
        for i in free:
            addition = min(limit - counts[i], max(1, budget * loads[i] // whole), spare)
            counts[i] = counts[i] + addition
            spare = spare - addition
    return np.array(counts)


def gaussian(stream_key, shape, deviation, most, pieces=(), kind=jnp.bfloat16):
    entries = deviation * jax.random.normal(stream_key, shape, jnp.float32)
    if pieces:
        entries = entries * block_scale(stream_key, shape, pieces, -0.22, 0.18)
    return jnp.clip(entries, -most, most).astype(kind)


def setup_inputs(seed: int = 0) -> dict:
    keys = jax.random.split(jax.random.key(seed), 6)
    grad_out = gaussian(keys[0], (TOKENS, D), 1.0, 6.0, ((0, 16),))
    gate_probs = jnp.clip(jnp.exp(math.log(1.0) - 2.9996462 * jax.random.uniform(keys[1], (TOKENS, TOP), jnp.float32) ** block_scale(keys[1], (TOKENS, TOP), ((0, 16),), -0.2, 0.2)), 0.049804688, 1.0).astype(jnp.bfloat16)
    expert_ids_keys = jax.random.split(jax.random.fold_in(keys[2], 1), TOKENS // TOK_DEV)
    expert_ids_turns = jax.random.permutation(jax.random.fold_in(keys[2], 3), TOKENS // TOK_DEV)
    expert_ids = jax.vmap(lambda own, number: deal_out(jax.random.fold_in(keys[2], 2), own, number, TOK_DEV, EXPERTS, TOP, CAP, 2))(expert_ids_keys, expert_ids_turns).reshape((TOKENS, TOP))
    saved_hidden = gaussian(keys[3], (EXPERTS, FF, ROWS), 1.0, 6.0, ((0, 16), (1, 32)))
    down_weight = gaussian(keys[4], (EXPERTS, FF, D), FF ** -0.5, 0.078125, ((0, 16), (1, 32)))
    return dict(grad_out=grad_out, gate_probs=gate_probs, expert_ids=expert_ids, saved_hidden=saved_hidden, down_weight=down_weight)


def positions(ids_flat, experts):
    onehot = (ids_flat[..., None] == jnp.arange(experts, dtype=jnp.int32)).astype(jnp.int32)
    before = jnp.cumsum(onehot, axis=-2) - onehot
    return jnp.sum(before * onehot, axis=-1).astype(jnp.int32)


def per_expert(operands):
    hidden, weight, slot_grad, slot_dy = operands
    grad_hid = lax.dot_general(weight, slot_grad, (((1,), (1,)), ((), ())), preferred_element_type=jnp.float32).astype(jnp.bfloat16)
    grad_weight = jnp.dot(hidden, slot_grad, preferred_element_type=jnp.float32).astype(jnp.bfloat16)
    expert_out = lax.dot_general(hidden, weight, (((0,), (0,)), ((), ())), preferred_element_type=jnp.float32)
    row_scores = jnp.sum(slot_dy.astype(jnp.float32) * expert_out, axis=1)
    return grad_hid, grad_weight, row_scores


def reference(grad_out, gate_probs, expert_ids, saved_hidden, down_weight):
    blocks = expert_ids.reshape(N_EXPERT, TOK_DEV * TOP)
    position = positions(blocks, EXPERTS)
    slot_row = (jnp.arange(N_EXPERT, dtype=jnp.int32)[:, None] * CAP + position).reshape(-1).astype(jnp.int32)
    expert_of = expert_ids.reshape(-1).astype(jnp.int32)
    dy_assign = jnp.repeat(grad_out, TOP, axis=0)
    prob_assign = gate_probs.reshape(-1).astype(jnp.float32)
    grad_assign = (prob_assign[:, None] * dy_assign.astype(jnp.float32)).astype(jnp.bfloat16)
    grad_slots = jnp.zeros((EXPERTS, ROWS, D), jnp.bfloat16).at[expert_of, slot_row].set(grad_assign)
    dy_slots = jnp.zeros((EXPERTS, ROWS, D), jnp.bfloat16).at[expert_of, slot_row].set(dy_assign)
    grad_hidden, grad_down, slot_score = lax.map(per_expert, (saved_hidden, down_weight, grad_slots, dy_slots))
    grad_gates = slot_score[expert_of, slot_row].reshape(TOKENS, TOP)
    return grad_hidden, grad_down, grad_gates
```

```python
import functools

import jax
import jax.numpy as jnp
from jax import lax
from jax.experimental import pallas as pl
from jax.experimental.pallas import tpu as pltpu
from jax.sharding import PartitionSpec as P

MESH = pl.DeviceIdType.MESH
NX, NY, NR = 4, 8, 4
NE = 16
TOK, TOP, CAP = 64, 4, 32
CH = 16
ORDER = (0, 1, 3, 2)
PLANE = NY * NR
F32, BF16 = jnp.float32, jnp.bfloat16


def kernel(
    ids_ref, gates_ref, tok_hbm, hid_hbm, w_hbm,
    gh_hbm, gd_hbm, score_ref,
    rows, w, hid, spread, gh, gd, before, meta, part, sc1, sc2,
    load_sem, out_sem, ss, rs, ds, rd, meta_s, meta_r, s1_s, s1_r, s2_s, s2_r,
):
    e, y, r = lax.axis_index("expert"), lax.axis_index("shard"), lax.axis_index("replica")
    x, half, core = e // 4, (e // 2) % 2, e % 2
    plane = y * NR + r
    cls = (y + 2 * r) % 4

    def expert(xx, hh, cc):
        return xx * 4 + hh * 2 + cc

    x1 = (expert((x + 1) % NX, half, core), y, r)
    x3 = (expert((x + 3) % NX, half, core), y, r)
    x2 = (expert((x + 2) % NX, half, core), y, r)
    y1, y7 = (e, (y + 1) % NY, r), (e, (y + 7) % NY, r)
    zn = (e, y, r + 1 - 2 * (r % 2))
    mirror = (expert(x, 1 - half, core), y, NR - 1 - r)
    twin = (expert(x, half, 1 - core), y, r)

    own_row = pl.multiple_of(e * TOK, TOK)
    load_tok = pltpu.make_async_copy(tok_hbm, rows.at[pl.ds(own_row, TOK)], load_sem.at[0])
    load_w = pltpu.make_async_copy(w_hbm, w, load_sem.at[1])
    load_h = pltpu.make_async_copy(hid_hbm, hid, load_sem.at[2])
    load_tok.start()

    barrier = pltpu.get_barrier_semaphore()
    for k in range(1, NE):
        pl.semaphore_signal(barrier, inc=1, device_id=((e + k) % NE, y, r), device_id_type=MESH)

    def greet(k, _):
        p = (plane + k) % PLANE
        pl.semaphore_signal(barrier, inc=1, device_id=(e, p // NR, p % NR), device_id_type=MESH)
        return 0

    lax.fori_loop(1, PLANE, greet, 0)
    pl.semaphore_signal(barrier, inc=1, device_id=mirror, device_id_type=MESH)
    load_w.start()
    load_h.start()

    place = (
        lax.broadcasted_iota(jnp.int32, (TOK, 128), 1)
        == lax.broadcasted_iota(jnp.int32, (TOK, 128), 0) + TOK * core
    ).astype(F32).astype(BF16)
    turned = (((0,), (0,)), ((), ()))
    meta[e, 0:4, :] = lax.dot_general(ids_ref[...].astype(F32).astype(BF16), place, turned, preferred_element_type=F32)
    meta[e, 4:8, :] = lax.dot_general(gates_ref[...], place, turned, preferred_element_type=F32)
    t_from = lax.broadcasted_iota(jnp.int32, (256, 256), 0)
    t_to = lax.broadcasted_iota(jnp.int32, (256, 256), 1)
    before[...] = ((t_from < t_to) & (t_from // TOK == t_to // TOK)).astype(F32).astype(BF16)

    pl.semaphore_wait(barrier, NE - 1 + PLANE - 1 + 1)

    sent, shared = [], []

    def block_row(h, dx, cc, k):
        b = expert((x + dx) % NX, half if h == 0 else 1 - half, cc)
        return pl.multiple_of(b * TOK + k * CH, CH)

    def arrival(h, dx, k):
        ref = rows.at[pl.ds(block_row(h, dx, core, k), CH)]
        return pltpu.make_async_remote_copy(
            src_ref=ref, dst_ref=ref, send_sem=ss.at[0], recv_sem=rs.at[h * 4 + dx, k], device_id=x1, device_id_type=MESH
        )

    def from_twin(h, dx, k):
        ref = rows.at[pl.ds(block_row(h, dx, 1 - core, k), CH)]
        return pltpu.make_async_remote_copy(
            src_ref=ref, dst_ref=ref, send_sem=ss.at[0], recv_sem=rd.at[h * 4 + dx, k], device_id=twin, device_id_type=MESH
        )

    def send(h, dx, k, to, there_h, there_dx):
        ref = rows.at[pl.ds(block_row(h, dx, core, k), CH)]
        copy = pltpu.make_async_remote_copy(
            src_ref=ref, dst_ref=ref, send_sem=ss.at[len(sent)], recv_sem=rs.at[there_h * 4 + there_dx, k],
            device_id=to, device_id_type=MESH,
        )
        copy.start()
        sent.append(copy)

    def share(h, dx, k):
        ref = rows.at[pl.ds(block_row(h, dx, core, k), CH)]
        copy = pltpu.make_async_remote_copy(
            src_ref=ref, dst_ref=ref, send_sem=ds.at[h * 4 + dx, k], recv_sem=rd.at[h * 4 + dx, k],
            device_id=twin, device_id_type=MESH,
        )
        copy.start()
        shared.append(copy)

    k0, k1, k2, k3 = cls, (cls + 1) % 4, (cls + 2) % 4, (cls + 3) % 4

    load_tok.wait()
    send(0, 0, k2, mirror, 1, 0)
    for to, dx in ((x1, 3), (x3, 1), (x2, 2)):
        send(0, 0, k0, to, 0, dx)
    for to, dx, kk in ((x1, 3, k2), (x3, 1, k2), (x1, 3, k3), (x3, 1, k1)):
        send(0, 0, kk, to, 0, dx)

    def meta_copy(k):
        other = (e + k) % NE
        return pltpu.make_async_remote_copy(
            src_ref=meta.at[e], dst_ref=meta.at[e], send_sem=meta_s.at[k], recv_sem=meta_r.at[e],
            device_id=(other, y, r), device_id_type=MESH,
        )

    for k in range(1, NE):
        meta_copy(k).start()
    for k in range(4):
        share(0, 0, k)

    arrival(1, 0, k0).wait_recv()
    for to, dx in ((x1, 3), (x3, 1), (x2, 2)):
        send(1, 0, k0, to, 1, dx)
    for to in (y1, y7, zn):
        send(1, 0, k0, to, 1, 0)
    share(1, 0, k0)
    arrival(0, 1, k0).wait_recv()
    send(0, 1, k0, y1, 0, 1)
    share(0, 1, k0)
    arrival(0, 3, k0).wait_recv()
    send(0, 3, k0, y7, 0, 3)
    share(0, 3, k0)
    arrival(0, 2, k0).wait_recv()
    for to in (y1, y7, zn):
        send(0, 2, k0, to, 0, 2)
    share(0, 2, k0)
    for dx in (1, 3, 2):
        arrival(1, dx, k0).wait_recv()
        for to in (y1, y7, zn):
            send(1, dx, k0, to, 1, dx)
        share(1, dx, k0)

    def take(h, dx, ks):
        for k in ks:
            arrival(h, dx, k).wait_recv()
            share(h, dx, k)

    load_w.wait()
    load_h.wait()
    for k in range(1, NE):
        other = (e + NE - k) % NE
        pltpu.make_async_remote_copy(
            src_ref=meta.at[other], dst_ref=meta.at[other], send_sem=meta_s.at[k], recv_sem=meta_r.at[other],
            device_id=(other, y, r), device_id_type=MESH,
        ).wait_recv()

    by_row = (((1,), (1,)), ((), ()))
    lane_block = lax.broadcasted_iota(jnp.int32, (1, 256), 1) // TOK
    scored = []
    for i, dx in enumerate(ORDER):
        if dx == 0:
            take(1, 0, (k1, k3, k2))
        else:
            take(0, dx, (k2, k1, k3) if dx != 3 else (k2, k3, k1))
            take(1, dx, (k1, k3, k2))
        for k in range(4):
            from_twin(0, dx, k).wait_recv()
            from_twin(1, dx, k).wait_recv()
        g = (x + dx) % NX
        here = pl.ds(pl.multiple_of(g * 256, 256), 256)
        slots = pl.ds(pl.multiple_of(g * 128, 128), 128)
        named = jnp.concatenate([meta[4 * g] + meta[4 * g + 1], meta[4 * g + 2] + meta[4 * g + 3]], axis=1)
        mine = named[0:4] == e.astype(F32)
        took = jnp.sum(mine.astype(F32), axis=0, keepdims=True)
        gate = jnp.sum(jnp.where(mine, named[4:8], 0.0), axis=0, keepdims=True)
        position = jnp.dot(
            jnp.broadcast_to(took, (8, 256)).astype(BF16), before[...], preferred_element_type=F32
        )[0:1]
        slot = jnp.where(took > 0.5, position.astype(jnp.int32) + lane_block * CAP, -1)
        pick = (lax.broadcasted_iota(jnp.int32, (128, 256), 0) == slot).astype(F32).astype(BF16)
        hs = jnp.dot(hid[:, slots], pick, preferred_element_type=F32)
        proj = lax.dot_general(w[...], rows[here, :], by_row, preferred_element_type=F32)
        score = jnp.sum(hs * proj, axis=0, keepdims=True)
        terms = jnp.where(mine, score, 0.0)
        for h in range(2):
            part[i, h, 0:4, :] = terms[:, 128 * h : 128 * h + 128]
            part[i, h, 4:8, :] = jnp.zeros((4, 128), F32)
        for h in range(2):
            for cc in range(2):
                there_h = half if h == 0 else 1 - half
                there_c = core if cc == 0 else 1 - core
                if dx == 0 and h == 0 and cc == 0:
                    continue
                copy = pltpu.make_async_remote_copy(
                    src_ref=part.at[i, there_h], dst_ref=sc1.at[e], send_sem=s1_s.at[i * 4 + h * 2 + cc],
                    recv_sem=s1_r.at[e], device_id=(expert(g, there_h, there_c), y, r), device_id_type=MESH,
                )
                copy.start()
                scored.append(copy)
        if dx == 0:
            sc1[e] = part[i, half]
        spread[:, here] = (hs * gate).astype(BF16)
        gh[:, slots] = lax.dot_general(
            (proj * gate).astype(BF16), pick, by_row, preferred_element_type=F32
        ).astype(BF16)

    out_h = pltpu.make_async_copy(gh, gh_hbm, out_sem.at[0])
    out_h.start()

    for k in range(1, NE):
        other = (e + k) % NE
        pltpu.make_async_remote_copy(
            src_ref=sc1.at[other], dst_ref=sc1.at[other], send_sem=s1_s.at[0], recv_sem=s1_r.at[other],
            device_id=(other, y, r), device_id_type=MESH,
        ).wait_recv()
    sc2[plane] = jnp.sum(sc1[...], axis=0)

    def plane_copy(k, at):
        p = (plane + k) % PLANE
        return pltpu.make_async_remote_copy(
            src_ref=sc2.at[at], dst_ref=sc2.at[at], send_sem=s2_s.at[k], recv_sem=s2_r.at[at],
            device_id=(e, p // NR, p % NR), device_id_type=MESH,
        )

    def tell(k, _):
        plane_copy(k, plane).start()
        return 0

    lax.fori_loop(1, PLANE, tell, 0)

    width = 512

    def weight_columns(j, _):
        cols = pl.ds(pl.multiple_of(j * width, width), width)
        gd[:, cols] = jnp.dot(spread[...], rows[:, cols], preferred_element_type=F32).astype(BF16)
        return 0

    lax.fori_loop(0, gd.shape[1] // width, weight_columns, 0)
    out_d = pltpu.make_async_copy(gd, gd_hbm, out_sem.at[1])
    out_d.start()

    def hear(k, _):
        plane_copy(k, (plane + k) % PLANE).wait_recv()
        return 0

    lax.fori_loop(1, PLANE, hear, 0)
    total = jnp.sum(sc2[...], axis=0)
    score_ref[...] = jnp.where(core == 0, total[:, 0:TOK], total[:, TOK : 2 * TOK])

    def told(k, _):
        plane_copy(k, plane).wait_send()
        return 0

    lax.fori_loop(1, PLANE, told, 0)
    for copy in sent + shared + scored:
        copy.wait_send()
    for k in range(1, NE):
        meta_copy(k).wait_send()
    out_h.wait()
    out_d.wait()


def shards(grad_out, gate_probs, expert_ids, saved_hidden, down_weight):
    hidden, weight = saved_hidden[0], down_weight[0]
    units, slots = hidden.shape
    width = weight.shape[1]
    dma = pltpu.SemaphoreType.DMA
    anywhere = pl.BlockSpec(memory_space=pl.ANY)
    vmem = pl.BlockSpec(memory_space=pltpu.VMEM)
    gh, gd, scores = pl.pallas_call(
        kernel,
        out_shape=(
            jax.ShapeDtypeStruct((units, slots), BF16),
            jax.ShapeDtypeStruct((units, width), BF16),
            jax.ShapeDtypeStruct((8, TOK), F32),
        ),
        in_specs=[vmem, vmem, anywhere, anywhere, anywhere],
        out_specs=(anywhere, anywhere, vmem),
        scratch_shapes=[
            pltpu.VMEM((NE * TOK, width), BF16),
            pltpu.VMEM((units, width), BF16),
            pltpu.VMEM((units, slots), BF16),
            pltpu.VMEM((units, NE * TOK), BF16),
            pltpu.VMEM((units, slots), BF16),
            pltpu.VMEM((units, width), BF16),
            pltpu.VMEM((256, 256), BF16),
            pltpu.VMEM((NE, 8, 128), F32),
            pltpu.VMEM((NX, 2, 8, 128), F32),
            pltpu.VMEM((NE, 8, 128), F32),
            pltpu.VMEM((PLANE, 8, 128), F32),
            dma((3,)),
            dma((2,)),
            dma((28,)),
            dma((8, 4)),
            dma((8, 4)),
            dma((8, 4)),
            dma((NE,)),
            dma((NE,)),
            dma((NE,)),
            dma((NE,)),
            dma((PLANE,)),
            dma((PLANE,)),
        ],
        compiler_params=pltpu.CompilerParams(collective_id=0, has_side_effects=True, vmem_limit_bytes=40 * 2**20),
        cost_estimate=pl.CostEstimate(
            flops=4 * units * width * NE * TOK, bytes_accessed=4 * units * width, transcendentals=0
        ),
    )(expert_ids, gate_probs, grad_out, hidden, weight)
    return gh[None], gd[None], scores[:TOP].T


def solution(mesh):
    split = P("expert", ("shard", "replica"), None)
    rows = P("expert", None)
    return jax.shard_map(
        shards, mesh=mesh, in_specs=(rows, rows, rows, split, split), out_specs=(split, split, rows), check_vma=False
    )
```

```python
import functools

import jax
import jax.numpy as jnp
from jax import lax
from jax.experimental import pallas as pl
from jax.experimental.pallas import tpu as pltpu
from jax.sharding import PartitionSpec as P

MESH = pl.DeviceIdType.MESH
NX, NY, NR = 4, 8, 4
NE = 16
TOK, TOP, CAP = 64, 4, 32
CH = 16
ORDER = (0, 1, 3, 2)
PLANE = NY * NR
F32, BF16 = jnp.float32, jnp.bfloat16


def kernel(
    ids_hbm, gates_hbm, tok_hbm, hid_hbm, w_hbm,
    gh_hbm, gd_hbm, score_ref,
    ids, gates, rows, w, hid, spread, gh, gd, before, meta, part, sc1, sc2,
    load_sem, out_sem, ss, rs, ds, rd, ms, mr, mds, mdr, s1_s, s1_r, s2_s, s2_r, wave, ready,
):
    e, y, r = lax.axis_index("expert"), lax.axis_index("shard"), lax.axis_index("replica")
    x, half, core = e // 4, (e // 2) % 2, e % 2
    plane = y * NR + r
    cls = (y + 2 * r) % 4

    def expert(xx, hh, cc):
        return xx * 4 + hh * 2 + cc

    x1 = (expert((x + 1) % NX, half, core), y, r)
    x3 = (expert((x + 3) % NX, half, core), y, r)
    x2 = (expert((x + 2) % NX, half, core), y, r)
    y1, y7 = (e, (y + 1) % NY, r), (e, (y + 7) % NY, r)
    zn = (e, y, r + 1 - 2 * (r % 2))
    far = (e, y, (r + 2) % NR)
    mirror = (expert(x, 1 - half, core), y, NR - 1 - r)
    twin = (expert(x, half, 1 - core), y, r)

    barrier = pltpu.get_barrier_semaphore()
    near = (x1, x3, x2, y1, y7, zn, far, twin)
    for other in near:
        pl.semaphore_signal(barrier, inc=1, device_id=other, device_id_type=MESH)

    @pl.when(half == 0)
    def _():
        pl.semaphore_signal(barrier, inc=1, device_id=mirror, device_id_type=MESH)

    own_row = pl.multiple_of(e * TOK, TOK)
    load_tok = pltpu.make_async_copy(tok_hbm, rows.at[pl.ds(own_row, TOK)], load_sem.at[0])
    load_w = pltpu.make_async_copy(w_hbm, w, load_sem.at[1])
    load_h = pltpu.make_async_copy(hid_hbm, hid, load_sem.at[2])
    load_ids = pltpu.make_async_copy(ids_hbm, ids, load_sem.at[3])
    load_gates = pltpu.make_async_copy(gates_hbm, gates, load_sem.at[4])
    load_tok.start()
    load_ids.start()
    load_gates.start()
    load_w.start()
    load_h.start()

    place = (
        lax.broadcasted_iota(jnp.int32, (TOK, 128), 1)
        == lax.broadcasted_iota(jnp.int32, (TOK, 128), 0) + TOK * core
    ).astype(F32).astype(BF16)
    load_ids.wait()
    load_gates.wait()
    meta[e, 0:4, :] = jnp.dot(ids[...].astype(F32).astype(BF16), place, preferred_element_type=F32)
    meta[e, 4:8, :] = jnp.dot(gates[...], place, preferred_element_type=F32)
    pl.semaphore_wait(barrier, len(near) + half)

    @pl.when(half == 1)
    def _():
        pl.semaphore_signal(ready, inc=1, device_id=mirror, device_id_type=MESH)

    def ripple(n, *others):
        for other in others:
            pl.semaphore_signal(wave.at[n], inc=1, device_id=other, device_id_type=MESH)

    ripple(0, y1, y7)

    sent, shared = [], []

    def block_row(h, dx, cc, k):
        b = expert((x + dx) % NX, half if h == 0 else 1 - half, cc)
        return pl.multiple_of(b * TOK + k * CH, CH)

    def arrival(h, dx, k):
        ref = rows.at[pl.ds(block_row(h, dx, core, k), CH)]
        return pltpu.make_async_remote_copy(
            src_ref=ref, dst_ref=ref, send_sem=ss.at[0], recv_sem=rs.at[h * 4 + dx, k], device_id=x1, device_id_type=MESH
        )

    def from_twin(h, dx, k):
        ref = rows.at[pl.ds(block_row(h, dx, 1 - core, k), CH)]
        return pltpu.make_async_remote_copy(
            src_ref=ref, dst_ref=ref, send_sem=ss.at[0], recv_sem=rd.at[h * 4 + dx, k], device_id=twin, device_id_type=MESH
        )

    def send(h, dx, k, to, there_h, there_dx):
        ref = rows.at[pl.ds(block_row(h, dx, core, k), CH)]
        copy = pltpu.make_async_remote_copy(
            src_ref=ref, dst_ref=ref, send_sem=ss.at[len(sent)], recv_sem=rs.at[there_h * 4 + there_dx, k],
            device_id=to, device_id_type=MESH,
        )
        copy.start()
        sent.append(copy)

    def share(h, dx, k):
        ref = rows.at[pl.ds(block_row(h, dx, core, k), CH)]
        copy = pltpu.make_async_remote_copy(
            src_ref=ref, dst_ref=ref, send_sem=ds.at[h * 4 + dx, k], recv_sem=rd.at[h * 4 + dx, k],
            device_id=twin, device_id_type=MESH,
        )
        copy.start()
        shared.append(copy)

    def meta_copy(h, dx, to, n, there_h, there_dx, send_sem, recv_sem, cc):
        ref = meta.at[expert((x + dx) % NX, half if h == 0 else 1 - half, cc)]
        return pltpu.make_async_remote_copy(
            src_ref=ref, dst_ref=ref, send_sem=send_sem.at[n], recv_sem=recv_sem.at[there_h * 4 + there_dx],
            device_id=to, device_id_type=MESH,
        )

    noted = []

    def note(h, dx, to, there_h, there_dx):
        copy = meta_copy(h, dx, to, len(noted), there_h, there_dx, ms, mr, core)
        copy.start()
        noted.append(copy)

    def note_twin(h, dx):
        copy = meta_copy(h, dx, twin, h * 4 + dx, h, dx, mds, mdr, core)
        copy.start()
        shared.append(copy)

    def noted_here(h, dx):
        meta_copy(h, dx, twin, 0, h, dx, ms, mr, core).wait_recv()
        note_twin(h, dx)

    def noted_by_twin(h, dx):
        meta_copy(h, dx, twin, 0, h, dx, mds, mdr, 1 - core).wait_recv()

    k0, k1, k2, k3 = cls, (cls + 1) % 4, (cls + 2) % 4, (cls + 3) % 4
    along = ((x1, 3), (x3, 1), (x2, 2))

    load_tok.wait()
    for to, dx in along:
        send(0, 0, k0, to, 0, dx)
    for to, dx in along:
        note(0, 0, to, 0, dx)

    @pl.when(half == 0)
    def _():
        pl.semaphore_wait(ready, 1)

    send(0, 0, k2, mirror, 1, 0)
    note(0, 0, mirror, 1, 0)
    note_twin(0, 0)
    for k in range(4):
        share(0, 0, k)
    send(0, 0, k2, x1, 0, 3)
    send(0, 0, k2, x3, 0, 1)

    t_from = lax.broadcasted_iota(jnp.int32, (256, 256), 0)
    t_to = lax.broadcasted_iota(jnp.int32, (256, 256), 1)
    before[...] = ((t_from < t_to) & (t_from // TOK == t_to // TOK)).astype(F32).astype(BF16)

    arrival(0, 1, k0).wait_recv()
    send(0, 1, k0, y1, 0, 1)
    share(0, 1, k0)
    arrival(0, 3, k0).wait_recv()
    send(0, 3, k0, y7, 0, 3)
    share(0, 3, k0)
    arrival(0, 2, k0).wait_recv()
    for to in (y1, y7, zn):
        send(0, 2, k0, to, 0, 2)
    share(0, 2, k0)
    for dx in (1, 3, 2):
        noted_here(0, dx)
    pl.semaphore_wait(wave.at[0], 2)
    ripple(1, y1, y7)

    arrival(1, 0, k0).wait_recv()
    for to, dx in along:
        send(1, 0, k0, to, 1, dx)
    for to in (y1, y7, zn):
        send(1, 0, k0, to, 1, 0)
    share(1, 0, k0)
    noted_here(1, 0)
    for to, dx in along:
        note(1, 0, to, 1, dx)
    send(0, 0, k3, x1, 0, 3)
    send(0, 0, k1, x3, 0, 1)
    pl.semaphore_wait(wave.at[1], 2)
    ripple(2, y1, y7)
    for dx in (1, 3, 2):
        arrival(1, dx, k0).wait_recv()
        for to in (y1, y7, zn):
            send(1, dx, k0, to, 1, dx)
        share(1, dx, k0)
    for dx in (1, 3, 2):
        noted_here(1, dx)
    pl.semaphore_wait(wave.at[2], 2)
    ripple(3, zn)

    def take(h, dx, ks):
        for k in ks:
            arrival(h, dx, k).wait_recv()
            share(h, dx, k)

    load_w.wait()
    load_h.wait()
    def bring(dx):
        take(0, dx, (k2, k1, k3) if dx == 2 else ((k2, k1, k3) if dx == 1 else (k2, k3, k1)))
        take(1, dx, (k1, k3, k2))

    by_row = (((1,), (1,)), ((), ()))
    lane_block = lax.broadcasted_iota(jnp.int32, (1, 256), 1) // TOK
    scored = []
    for i, dx in enumerate(ORDER):
        if i == 0:
            take(1, 0, (k1, k3, k2))
            bring(1)
            pl.semaphore_wait(wave.at[3], 1)
            ripple(4, far)
        elif i < 3:
            bring(ORDER[i + 1])
        for k in range(4):
            from_twin(0, dx, k).wait_recv()
            from_twin(1, dx, k).wait_recv()
        noted_by_twin(0, dx)
        noted_by_twin(1, dx)
        g = (x + dx) % NX
        here = pl.ds(pl.multiple_of(g * 256, 256), 256)
        slots = pl.ds(pl.multiple_of(g * 128, 128), 128)
        named = jnp.concatenate([meta[4 * g] + meta[4 * g + 1], meta[4 * g + 2] + meta[4 * g + 3]], axis=1)
        mine = named[0:4] == e.astype(F32)
        took = jnp.sum(mine.astype(F32), axis=0, keepdims=True)
        gate = jnp.sum(jnp.where(mine, named[4:8], 0.0), axis=0, keepdims=True)
        position = jnp.dot(
            jnp.broadcast_to(took, (8, 256)).astype(BF16), before[...], preferred_element_type=F32
        )[0:1]
        slot = jnp.where(took > 0.5, position.astype(jnp.int32) + lane_block * CAP, -1)
        pick = (lax.broadcasted_iota(jnp.int32, (128, 256), 0) == slot).astype(F32).astype(BF16)
        hs = jnp.dot(hid[:, slots], pick, preferred_element_type=F32)
        proj = lax.dot_general(w[...], rows[here, :], by_row, preferred_element_type=F32)
        score = jnp.sum(hs * proj, axis=0, keepdims=True)
        terms = jnp.where(mine, score, 0.0)
        for h in range(2):
            part[i, h, 0:4, :] = terms[:, 128 * h : 128 * h + 128]
            part[i, h, 4:8, :] = jnp.zeros((4, 128), F32)
        for h in range(2):
            for cc in range(2):
                there_h = half if h == 0 else 1 - half
                there_c = core if cc == 0 else 1 - core
                if dx == 0 and h == 0 and cc == 0:
                    continue
                copy = pltpu.make_async_remote_copy(
                    src_ref=part.at[i, there_h], dst_ref=sc1.at[e], send_sem=s1_s.at[i * 4 + h * 2 + cc],
                    recv_sem=s1_r.at[e], device_id=(expert(g, there_h, there_c), y, r if h == 0 else NR - 1 - r),
                    device_id_type=MESH,
                )
                copy.start()
                scored.append(copy)
        if dx == 0:
            sc1[e] = part[i, half]
        spread[:, here] = (hs * gate).astype(BF16)
        gh[:, slots] = lax.dot_general(
            (proj * gate).astype(BF16), pick, by_row, preferred_element_type=F32
        ).astype(BF16)

    out_h = pltpu.make_async_copy(gh, gh_hbm, out_sem.at[0])
    out_h.start()

    for k in range(1, NE):
        other = (e + k) % NE
        pltpu.make_async_remote_copy(
            src_ref=sc1.at[other], dst_ref=sc1.at[other], send_sem=s1_s.at[0], recv_sem=s1_r.at[other],
            device_id=(other, y, r), device_id_type=MESH,
        ).wait_recv()
    sc2[plane] = jnp.sum(sc1[...], axis=0)

    def plane_copy(k, at):
        p = (plane + k) % PLANE
        return pltpu.make_async_remote_copy(
            src_ref=sc2.at[at], dst_ref=sc2.at[at], send_sem=s2_s.at[k], recv_sem=s2_r.at[at],
            device_id=(e, p // NR, p % NR), device_id_type=MESH,
        )

    def tell(k, _):
        plane_copy(k, plane).start()
        return 0

    pl.semaphore_wait(wave.at[4], 1)
    lax.fori_loop(1, PLANE, tell, 0)

    width = 512

    def weight_columns(j, _):
        cols = pl.ds(pl.multiple_of(j * width, width), width)
        gd[:, cols] = jnp.dot(spread[...], rows[:, cols], preferred_element_type=F32).astype(BF16)
        return 0

    lax.fori_loop(0, gd.shape[1] // width, weight_columns, 0)
    out_d = pltpu.make_async_copy(gd, gd_hbm, out_sem.at[1])
    out_d.start()

    def hear(k, _):
        plane_copy(k, (plane + k) % PLANE).wait_recv()
        return 0

    lax.fori_loop(1, PLANE, hear, 0)
    total = jnp.sum(sc2[...], axis=0)
    score_ref[...] = jnp.where(core == 0, total[0:TOP, 0:TOK], total[0:TOP, TOK : 2 * TOK])

    def told(k, _):
        plane_copy(k, plane).wait_send()
        return 0

    lax.fori_loop(1, PLANE, told, 0)
    for copy in sent + shared + scored + noted:
        copy.wait_send()
    out_h.wait()
    out_d.wait()


def shards(grad_out, gate_probs, expert_ids, saved_hidden, down_weight):
    hidden, weight = saved_hidden[0], down_weight[0]
    units, slots = hidden.shape
    width = weight.shape[1]
    dma = pltpu.SemaphoreType.DMA
    anywhere = pl.BlockSpec(memory_space=pl.ANY)
    vmem = pl.BlockSpec(memory_space=pltpu.VMEM)
    hbm = pl.BlockSpec(memory_space=pltpu.HBM)
    gh, gd, scores = pl.pallas_call(
        kernel,
        out_shape=(
            jax.ShapeDtypeStruct((units, slots), BF16),
            jax.ShapeDtypeStruct((units, width), BF16),
            jax.ShapeDtypeStruct((TOP, TOK), F32),
        ),
        in_specs=[hbm] * 5,
        out_specs=(anywhere, anywhere, vmem),
        scratch_shapes=[
            pltpu.VMEM((TOP, TOK), jnp.int32),
            pltpu.VMEM((TOP, TOK), BF16),
            pltpu.VMEM((NE * TOK, width), BF16),
            pltpu.VMEM((units, width), BF16),
            pltpu.VMEM((units, slots), BF16),
            pltpu.VMEM((units, NE * TOK), BF16),
            pltpu.VMEM((units, slots), BF16),
            pltpu.VMEM((units, width), BF16),
            pltpu.VMEM((256, 256), BF16),
            pltpu.VMEM((NE, 8, 128), F32),
            pltpu.VMEM((NX, 2, 8, 128), F32),
            pltpu.VMEM((NE, 8, 128), F32),
            pltpu.VMEM((PLANE, 8, 128), F32),
            dma((5,)),
            dma((2,)),
            dma((28,)),
            dma((8, 4)),
            dma((8, 4)),
            dma((8, 4)),
            dma((7,)),
            dma((8,)),
            dma((8,)),
            dma((8,)),
            dma((NE,)),
            dma((NE,)),
            dma((PLANE,)),
            dma((PLANE,)),
            pltpu.SemaphoreType.REGULAR((5,)),
            pltpu.SemaphoreType.REGULAR,
        ],
        compiler_params=pltpu.CompilerParams(collective_id=0, has_side_effects=True, vmem_limit_bytes=40 * 2**20),
        cost_estimate=pl.CostEstimate(
            flops=4 * units * width * NE * TOK, bytes_accessed=4 * units * width, transcendentals=0
        ),
    )(*(pltpu.with_memory_space_constraint(a, pltpu.HBM) for a in (expert_ids.T, gate_probs.T, grad_out, hidden, weight)))
    return gh[None], gd[None], scores.T


def solution(mesh):
    split = P("expert", ("shard", "replica"), None)
    rows = P("expert", None)
    return jax.shard_map(
        shards, mesh=mesh, in_specs=(rows, rows, rows, split, split), out_specs=(split, split, rows), check_vma=False
    )
```

```python
import functools

import jax
import jax.numpy as jnp
from jax import lax
from jax.experimental import pallas as pl
from jax.experimental.pallas import tpu as pltpu
from jax.sharding import PartitionSpec as P

MESH = pl.DeviceIdType.MESH
NX, NY, NR = 4, 8, 4
NE = 16
TOK, TOP, CAP = 64, 4, 32
CH = 16
STRIPS = 2
PLANE = NY * NR
F32, BF16 = jnp.float32, jnp.bfloat16


def kernel(
    ids_hbm, gates_hbm, tok_hbm, hid_hbm, w_hbm,
    gh_hbm, gd_hbm, score_hbm,
    scores, ids, gates, rows, w, hid, spread, hs, scaled, pick, mine, gate, gh, gd, before, meta, part, sc1, sc2,
    load_sem, out_sem, ss, rs, rb, ds, rd, ms, mr, mds, mdr, s1_s, s1_r, s2_s, s2_r, wave, ready,
):
    e, y, r = lax.axis_index("expert"), lax.axis_index("shard"), lax.axis_index("replica")
    x, half, core = e // 4, (e // 2) % 2, e % 2
    plane = y * NR + r
    cls = (y + 2 * r) % 4

    def expert(xx, hh, cc):
        return xx * 4 + hh * 2 + cc

    def block(xx, hh, cc):
        return hh * 8 + xx * 2 + cc

    own = block(x, half, core)
    x1 = (expert((x + 1) % NX, half, core), y, r)
    x3 = (expert((x + 3) % NX, half, core), y, r)
    x2 = (expert((x + 2) % NX, half, core), y, r)
    y1, y7 = (e, (y + 1) % NY, r), (e, (y + 7) % NY, r)
    zn = (e, y, r + 1 - 2 * (r % 2))
    far = (e, y, (r + 2) % NR)
    mirror = (expert(x, 1 - half, core), y, NR - 1 - r)
    twin = (expert(x, half, 1 - core), y, r)

    barrier = pltpu.get_barrier_semaphore()
    near = (x1, x3, x2, y1, y7, zn, far, twin)
    for other in near:
        pl.semaphore_signal(barrier, inc=1, device_id=other, device_id_type=MESH)

    @pl.when(half == 0)
    def _():
        pl.semaphore_signal(barrier, inc=1, device_id=mirror, device_id_type=MESH)

    own_row = pl.multiple_of(own * TOK, TOK)
    load_tok = pltpu.make_async_copy(tok_hbm, rows.at[pl.ds(own_row, TOK)], load_sem.at[0])
    load_w = pltpu.make_async_copy(w_hbm, w, load_sem.at[1])
    load_h = pltpu.make_async_copy(hid_hbm, hid, load_sem.at[2])
    load_ids = pltpu.make_async_copy(ids_hbm, ids, load_sem.at[3])
    load_gates = pltpu.make_async_copy(gates_hbm, gates, load_sem.at[4])
    load_tok.start()
    load_ids.start()
    load_gates.start()
    load_w.start()
    load_h.start()

    place = (
        lax.broadcasted_iota(jnp.int32, (TOK, 128), 1)
        == lax.broadcasted_iota(jnp.int32, (TOK, 128), 0) + TOK * core
    ).astype(F32).astype(BF16)
    load_ids.wait()
    load_gates.wait()
    meta[own, 0:4, :] = jnp.dot(ids[...].astype(F32).astype(BF16), place, preferred_element_type=F32)
    meta[own, 4:8, :] = jnp.dot(gates[...], place, preferred_element_type=F32)
    pl.semaphore_wait(barrier, len(near) + half)

    @pl.when(half == 1)
    def _():
        pl.semaphore_signal(ready, inc=1, device_id=mirror, device_id_type=MESH)

    def ripple(n, *others):
        for other in others:
            pl.semaphore_signal(wave.at[n], inc=1, device_id=other, device_id_type=MESH)

    ripple(0, y1, y7)

    sent, shared = [], []

    def block_row(h, dx, cc, k):
        b = block((x + dx) % NX, half if h == 0 else 1 - half, cc)
        return pl.multiple_of(b * TOK + k * CH, CH)

    wide = rows.shape[1]
    whole = pl.ds(0, wide)
    strips = [pl.ds(n * (wide // STRIPS), wide // STRIPS) for n in range(STRIPS)]

    def arrival(h, dx, k, n=None):
        ref = rows.at[pl.ds(block_row(h, dx, core, k), CH), whole if n is None else strips[n]]
        sem = rs.at[h * 4 + dx, k] if n is None else rb.at[dx, n]
        return pltpu.make_async_remote_copy(
            src_ref=ref, dst_ref=ref, send_sem=ss, recv_sem=sem, device_id=x1, device_id_type=MESH
        )

    def from_twin(h, dx):
        ref = rows.at[pl.ds(block_row(h, dx, 1 - core, 0), TOK)]
        pltpu.make_async_remote_copy(
            src_ref=ref, dst_ref=ref, send_sem=ss, recv_sem=rd.at[h * 4 + dx], device_id=twin, device_id_type=MESH
        ).wait_recv()

    def outgoing(h, dx, k, to, there_h, there_dx, n=None, first=False):
        ref = rows.at[pl.ds(block_row(h, dx, core, k), CH), whole if n is None else strips[n]]
        sem = rb.at[there_dx, n] if first else rs.at[there_h * 4 + there_dx, k]
        copy = pltpu.make_async_remote_copy(
            src_ref=ref, dst_ref=ref, send_sem=ss, recv_sem=sem, device_id=to, device_id_type=MESH
        )
        sent.append(CH if n is None else CH / STRIPS)
        return copy

    def send(*what, **how):
        outgoing(*what, **how).start()

    def share(h, dx, k, count=1):
        ref = rows.at[pl.ds(block_row(h, dx, core, k), CH * count)]
        copy = pltpu.make_async_remote_copy(
            src_ref=ref, dst_ref=ref, send_sem=ds, recv_sem=rd.at[h * 4 + dx],
            device_id=twin, device_id_type=MESH,
        )
        copy.start()
        shared.append(CH * count)

    def meta_copy(h, dx, to, send_sem, recv_sem, cc):
        ref = meta.at[block((x + dx) % NX, half if h == 0 else 1 - half, cc)]
        return pltpu.make_async_remote_copy(
            src_ref=ref, dst_ref=ref, send_sem=send_sem, recv_sem=recv_sem, device_id=to, device_id_type=MESH
        )

    noted = []

    def note(h, dx, to, there_h, there_dx):
        copy = meta_copy(h, dx, to, ms, mr.at[there_h * 4 + there_dx], core)
        copy.start()
        noted.append(copy)

    def note_twin(h, dx):
        meta_copy(h, dx, twin, mds, mdr, core).start()

    def noted_here(h, dx):
        meta_copy(h, dx, twin, ms, mr.at[h * 4 + dx], core).wait_recv()
        note_twin(h, dx)

    def all_of(ref, count, send_sem, recv_sem):
        some = ref.at[pl.ds(0, count)]
        return pltpu.make_async_remote_copy(
            src_ref=some, dst_ref=some, send_sem=send_sem, recv_sem=recv_sem, device_id=twin, device_id_type=MESH
        )

    def prepare():
        all_of(meta, 8, mds, mdr).wait_recv()
        named = jnp.concatenate([meta[2 * n] + meta[2 * n + 1] for n in range(NE // 2)], axis=1)
        is_mine = (named[0:4] == e.astype(F32)).astype(F32)
        took = jnp.sum(is_mine, axis=0, keepdims=True)
        its_gate = jnp.sum(is_mine * named[4:8], axis=0, keepdims=True)
        groups = [slice(256 * g, 256 * g + 256) for g in range(NX)]
        by_group = jnp.concatenate([took[:, here] for here in groups] + [jnp.zeros((4, 256), F32)], axis=0)
        position = jnp.dot(by_group.astype(BF16), before[...], preferred_element_type=F32)
        lane, line = (lax.broadcasted_iota(jnp.int32, (8, 256), d) for d in (1, 0))
        first_slot = lane // 128 * 128 + line // 2 * 64 + lane // TOK % 2 * CAP
        slot = jnp.where(by_group > 0.5, position.astype(jnp.int32) + first_slot, -1)
        slot_row = lax.broadcasted_iota(jnp.int32, (256, 256), 0)
        picked = [(slot_row == slot[g : g + 1]).astype(F32).astype(BF16) for g in range(NX)]
        of_tokens = [
            jnp.dot(hid[:, 256 * (g % 2) : 256 * (g % 2) + 256], picked[g], preferred_element_type=F32)
            for g in range(NX)
        ]
        mine[...] = jnp.concatenate([is_mine, jnp.zeros((4, NE * TOK), F32)], axis=0)
        gate[...] = jnp.broadcast_to(its_gate, (8, NE * TOK))
        for g, here in enumerate(groups):
            pick[g] = picked[g]
            hs[:, here] = of_tokens[g].astype(BF16)
            spread[:, here] = (of_tokens[g] * its_gate[:, here]).astype(BF16)

    k0, k1, k2, k3 = cls, (cls + 1) % 4, (cls + 2) % 4, (cls + 3) % 4
    along = ((x1, 3), (x3, 1), (x2, 2))

    load_tok.wait()
    for to, dx in along:
        note(0, 0, to, 0, dx)
        send(0, 0, k0, to, 0, dx)
    crossing = [meta_copy(0, 0, mirror, ms, mr.at[4], core)]
    noted.append(crossing[0])
    crossing += [outgoing(0, 0, k2, mirror, 1, 0, n, first=True) for n in range(STRIPS)]

    @pl.when(half == 0)
    def _():
        pl.semaphore_wait(ready, 1)

    for copy in crossing:
        copy.start()
    note_twin(0, 0)
    share(0, 0, 0, 4)
    send(0, 0, k2, x1, 0, 3)
    send(0, 0, k2, x3, 0, 1)

    t_from = lax.broadcasted_iota(jnp.int32, (256, 256), 0)
    t_to = lax.broadcasted_iota(jnp.int32, (256, 256), 1)
    before[...] = ((t_from < t_to) & (t_from // TOK == t_to // TOK)).astype(F32).astype(BF16)

    arrival(0, 2, k0).wait_recv()
    for to in (y1, y7, zn):
        send(0, 2, k0, to, 0, 2)
    share(0, 2, k0)
    for dx in (1, 3, 2):
        noted_here(0, dx)
    pl.semaphore_wait(wave.at[0], 2)
    ripple(1, y1, y7)

    noted_here(1, 0)
    for to, dx in along:
        note(1, 0, to, 1, dx)
    for n in range(STRIPS):
        arrival(1, 0, k0, n).wait_recv()
        for to, dx in along:
            send(1, 0, k0, to, 1, dx, n, first=True)
        for to in (y1, y7, zn):
            send(1, 0, k0, to, 1, 0, n)
    for kk in (k1, k3):
        send(0, 0, kk, x1, 0, 3)
        send(0, 0, kk, x3, 0, 1)
    share(1, 0, k0)
    for dx in (1, 3, 2):
        noted_here(1, dx)
    pl.semaphore_wait(wave.at[1], 2)
    ripple(2, y1, y7)
    for dx in (1, 3):
        arrival(0, dx, k0).wait_recv()
        share(0, dx, k0)
    for n in range(STRIPS):
        for dx in (1, 3, 2):
            arrival(1, dx, k0, n).wait_recv()
            for to in (y1, y7, zn):
                send(1, dx, k0, to, 1, dx, n)
    for dx in (1, 3, 2):
        share(1, dx, k0)
    pl.semaphore_wait(wave.at[2], 2)
    ripple(3, zn)

    load_h.wait()
    prepare()
    load_w.wait()

    def bring(h, dx):
        for k in (k2, k1, k3):
            arrival(h, dx, k).wait_recv()
            share(h, dx, k)

    by_row = (((1,), (1,)), ((), ()))
    scored = []

    def multiply(i):
        hh = half if i == 0 else 1 - half
        for dx in range(NX):
            if (i, dx) != (0, 0):
                from_twin(i, dx)
        here = pl.ds(pl.multiple_of(hh * 512, 512), 512)
        proj = lax.dot_general(w[...], rows[here, :], by_row, preferred_element_type=F32)
        terms = mine[:, here] * jnp.sum(hs[:, here].astype(F32) * proj, axis=0, keepdims=True)
        for n in range(NX):
            part[i, n] = terms[:, 128 * n : 128 * n + 128]
        for dx in (2, 1, 3, 0):
            xx = (x + dx) % NX
            for cc in range(2):
                if (i, dx, cc) == (0, 0, 0):
                    continue
                copy = pltpu.make_async_remote_copy(
                    src_ref=part.at[i, xx], dst_ref=sc1.at[e], send_sem=s1_s, recv_sem=s1_r,
                    device_id=(expert(xx, hh, core if cc == 0 else 1 - core), y, r if i == 0 else NR - 1 - r),
                    device_id_type=MESH,
                )
                copy.start()
                scored.append(copy)
        if i == 0:
            sc1[e] = part[0, x]
        scaled[:, here] = (proj * gate[0:1, here]).astype(BF16)

    for dx in (2, 1, 3):
        bring(0, dx)
    bring(1, 0)
    pl.semaphore_wait(wave.at[3], 1)
    ripple(4, far)
    from_twin(0, 0)
    multiply(0)
    for dx in (1, 3, 2):
        bring(1, dx)
    multiply(1)

    for n in range(2):
        slots = slice(256 * n, 256 * n + 256)
        gh[:, slots] = sum(
            lax.dot_general(scaled[:, 256 * g : 256 * g + 256], pick[g], by_row, preferred_element_type=F32)
            for g in (n, n + 2)
        ).astype(BF16)

    out_h = pltpu.make_async_copy(gh, gh_hbm, out_sem.at[0])
    out_h.start()

    width = 512

    def weight_columns(first, last):
        for j in range(first, last):
            cols = pl.ds(j * width, width)
            gd[:, cols] = jnp.dot(spread[...], rows[:, cols], preferred_element_type=F32).astype(BF16)

    weight_columns(0, 3)

    all_of(sc1, NE - 1, s1_s, s1_r).wait_recv()
    sc2[plane] = jnp.sum(sc1[...], axis=0)

    def tell(k, _):
        p = (plane + k) % PLANE
        pltpu.make_async_remote_copy(
            src_ref=sc2.at[plane], dst_ref=sc2.at[plane], send_sem=s2_s, recv_sem=s2_r,
            device_id=(e, p // NR, p % NR), device_id_type=MESH,
        ).start()
        return 0

    pl.semaphore_wait(wave.at[4], 1)
    lax.fori_loop(1, PLANE, tell, 0)

    weight_columns(3, gd.shape[1] // width)
    out_d = pltpu.make_async_copy(gd, gd_hbm, out_sem.at[1])
    out_d.start()

    assert len(noted) == 7 and len(scored) == NE - 1
    all_of(rows, int(sum(sent)), ss, ss).wait_send()
    all_of(rows, sum(shared), ds, ds).wait_send()
    all_of(meta, len(noted), ms, ms).wait_send()
    all_of(meta, 8, mds, mds).wait_send()
    all_of(sc1, len(scored), s1_s, s1_s).wait_send()
    out_h.wait()
    out_d.wait()
    exchange = all_of(sc2, PLANE - 1, s2_s, s2_r)
    exchange.wait_recv()
    total = jnp.sum(sc2[...], axis=0)
    scores[...] = jnp.where(core == 0, total[0:TOP, 0:TOK], total[0:TOP, TOK : 2 * TOK])
    out_s = pltpu.make_async_copy(scores, score_hbm, out_sem.at[2])
    out_s.start()
    exchange.wait_send()
    out_s.wait()


def shards(grad_out, gate_probs, expert_ids, saved_hidden, down_weight):
    hidden, weight = saved_hidden[0], down_weight[0]
    units, slots = hidden.shape
    width = weight.shape[1]
    dma = pltpu.SemaphoreType.DMA
    anywhere = pl.BlockSpec(memory_space=pl.ANY)
    hbm = pl.BlockSpec(memory_space=pltpu.HBM)
    gh, gd, scores = pl.pallas_call(
        kernel,
        out_shape=(
            jax.ShapeDtypeStruct((units, slots), BF16),
            jax.ShapeDtypeStruct((units, width), BF16),
            jax.ShapeDtypeStruct((TOP, TOK), F32),
        ),
        in_specs=[hbm] * 5,
        out_specs=(anywhere,) * 3,
        scratch_shapes=[
            pltpu.VMEM((TOP, TOK), F32),
            pltpu.VMEM((TOP, TOK), jnp.int32),
            pltpu.VMEM((TOP, TOK), BF16),
            pltpu.VMEM((NE * TOK, width), BF16),
            pltpu.VMEM((units, width), BF16),
            pltpu.VMEM((units, slots), BF16),
            pltpu.VMEM((units, NE * TOK), BF16),
            pltpu.VMEM((units, NE * TOK), BF16),
            pltpu.VMEM((units, NE * TOK), BF16),
            pltpu.VMEM((NX, 256, 256), BF16),
            pltpu.VMEM((8, NE * TOK), F32),
            pltpu.VMEM((8, NE * TOK), F32),
            pltpu.VMEM((units, slots), BF16),
            pltpu.VMEM((units, width), BF16),
            pltpu.VMEM((256, 256), BF16),
            pltpu.VMEM((NE, 8, 128), F32),
            pltpu.VMEM((2, NX, 8, 128), F32),
            pltpu.VMEM((NE, 8, 128), F32),
            pltpu.VMEM((PLANE, 8, 128), F32),
            dma((5,)),
            dma((3,)),
            dma,
            dma((8, 4)),
            dma((NX, STRIPS)),
            dma,
            dma((8,)),
            dma,
            dma((8,)),
            dma,
            dma,
            dma,
            dma,
            dma,
            dma,
            pltpu.SemaphoreType.REGULAR((5,)),
            pltpu.SemaphoreType.REGULAR,
        ],
        compiler_params=pltpu.CompilerParams(collective_id=0, has_side_effects=True, vmem_limit_bytes=40 * 2**20),
        cost_estimate=pl.CostEstimate(
            flops=4 * units * width * NE * TOK, bytes_accessed=4 * units * width, transcendentals=0
        ),
    )(*(pltpu.with_memory_space_constraint(a, pltpu.HBM) for a in (expert_ids.T, gate_probs.T, grad_out, hidden, weight)))
    return gh[None], gd[None], scores.T


def solution(mesh):
    split = P("expert", ("shard", "replica"), None)
    rows = P("expert", None)
    return jax.shard_map(
        shards, mesh=mesh, in_specs=(rows, rows, rows, split, split), out_specs=(split, split, rows), check_vma=False
    )
```

```python
import functools

import jax
import jax.numpy as jnp
from jax import lax
from jax.experimental import pallas as pl
from jax.experimental.pallas import tpu as pltpu
from jax.sharding import PartitionSpec as P

MESH = pl.DeviceIdType.MESH
NX, NY, NR = 4, 8, 4
NE = 16
TOK, TOP, CAP = 64, 4, 32
CH = 16
STRIPS = 2
PLANE = NY * NR
F32, BF16 = jnp.float32, jnp.bfloat16


def kernel(
    ids_hbm, gates_hbm, tok_hbm, hid_hbm, w_hbm,
    gh_hbm, gd_hbm, score_hbm,
    scores, ids, gates, rows, w, hid, spread, hs, scaled, pick, mine, gate, gh, gd, before, meta, part, sc1, sc2,
    load_sem, out_sem, ss, rs, rb, ds, rd, ms, mr, mds, mdr, s1_s, s1_r, s2_s, s2_r, wave, ready,
):
    e, y, r = lax.axis_index("expert"), lax.axis_index("shard"), lax.axis_index("replica")
    x, half, core = e // 4, (e // 2) % 2, e % 2
    plane = y * NR + r
    cls = (y + 2 * r) % 4

    def expert(xx, hh, cc):
        return xx * 4 + hh * 2 + cc

    def block(xx, hh, cc):
        return hh * 8 + xx * 2 + cc

    own = block(x, half, core)
    x1 = (expert((x + 1) % NX, half, core), y, r)
    x3 = (expert((x + 3) % NX, half, core), y, r)
    x2 = (expert((x + 2) % NX, half, core), y, r)
    y1, y7 = (e, (y + 1) % NY, r), (e, (y + 7) % NY, r)
    zn = (e, y, r + 1 - 2 * (r % 2))
    far = (e, y, (r + 2) % NR)
    mirror = (expert(x, 1 - half, core), y, NR - 1 - r)
    twin = (expert(x, half, 1 - core), y, r)

    barrier = pltpu.get_barrier_semaphore()
    near = (x1, x3, x2, y1, y7, zn, far, twin)
    for other in near:
        pl.semaphore_signal(barrier, inc=1, device_id=other, device_id_type=MESH)

    @pl.when(half == 0)
    def _():
        pl.semaphore_signal(barrier, inc=1, device_id=mirror, device_id_type=MESH)

    own_row = pl.multiple_of(own * TOK, TOK)
    load_tok = pltpu.make_async_copy(tok_hbm, rows.at[pl.ds(own_row, TOK)], load_sem.at[0])
    load_w = pltpu.make_async_copy(w_hbm, w, load_sem.at[1])
    load_h = pltpu.make_async_copy(hid_hbm, hid, load_sem.at[2])
    load_ids = pltpu.make_async_copy(ids_hbm, ids, load_sem.at[3])
    load_gates = pltpu.make_async_copy(gates_hbm, gates, load_sem.at[4])
    load_tok.start()
    load_ids.start()
    load_gates.start()
    load_w.start()
    load_h.start()

    place = (
        lax.broadcasted_iota(jnp.int32, (TOK, 128), 1)
        == lax.broadcasted_iota(jnp.int32, (TOK, 128), 0) + TOK * core
    ).astype(F32).astype(BF16)
    load_ids.wait()
    load_gates.wait()
    meta[own, 0:4, :] = jnp.dot(ids[...].astype(F32).astype(BF16), place, preferred_element_type=F32)
    meta[own, 4:8, :] = jnp.dot(gates[...], place, preferred_element_type=F32)
    pl.semaphore_wait(barrier, len(near) + half)

    @pl.when(half == 1)
    def _():
        pl.semaphore_signal(ready, inc=1, device_id=mirror, device_id_type=MESH)

    def ripple(n, *others):
        for other in others:
            pl.semaphore_signal(wave.at[n], inc=1, device_id=other, device_id_type=MESH)

    ripple(0, y1, y7)

    sent, shared = [], []

    def block_row(h, dx, cc, k):
        b = block((x + dx) % NX, half if h == 0 else 1 - half, cc)
        return pl.multiple_of(b * TOK + k * CH, CH)

    wide = rows.shape[1]
    whole = pl.ds(0, wide)
    strips = [pl.ds(n * (wide // STRIPS), wide // STRIPS) for n in range(STRIPS)]

    def arrival(h, dx, k, n=None):
        ref = rows.at[pl.ds(block_row(h, dx, core, k), CH), whole if n is None else strips[n]]
        sem = rs.at[h * 4 + dx, k] if n is None else rb.at[dx, n]
        return pltpu.make_async_remote_copy(
            src_ref=ref, dst_ref=ref, send_sem=ss, recv_sem=sem, device_id=x1, device_id_type=MESH
        )

    def from_twin(h, dx):
        ref = rows.at[pl.ds(block_row(h, dx, 1 - core, 0), TOK)]
        pltpu.make_async_remote_copy(
            src_ref=ref, dst_ref=ref, send_sem=ss, recv_sem=rd.at[h * 4 + dx], device_id=twin, device_id_type=MESH
        ).wait_recv()

    def outgoing(h, dx, k, to, there_h, there_dx, n=None, first=False):
        ref = rows.at[pl.ds(block_row(h, dx, core, k), CH), whole if n is None else strips[n]]
        sem = rb.at[there_dx, n] if first else rs.at[there_h * 4 + there_dx, k]
        copy = pltpu.make_async_remote_copy(
            src_ref=ref, dst_ref=ref, send_sem=ss, recv_sem=sem, device_id=to, device_id_type=MESH
        )
        sent.append(CH if n is None else CH / STRIPS)
        return copy

    def send(*what, **how):
        outgoing(*what, **how).start()

    def share(h, dx, k, count=1):
        ref = rows.at[pl.ds(block_row(h, dx, core, k), CH * count)]
        copy = pltpu.make_async_remote_copy(
            src_ref=ref, dst_ref=ref, send_sem=ds, recv_sem=rd.at[h * 4 + dx],
            device_id=twin, device_id_type=MESH,
        )
        copy.start()
        shared.append(CH * count)

    def meta_copy(h, dx, to, send_sem, recv_sem, cc):
        ref = meta.at[block((x + dx) % NX, half if h == 0 else 1 - half, cc)]
        return pltpu.make_async_remote_copy(
            src_ref=ref, dst_ref=ref, send_sem=send_sem, recv_sem=recv_sem, device_id=to, device_id_type=MESH
        )

    noted = []

    def note(h, dx, to, there_h, there_dx):
        copy = meta_copy(h, dx, to, ms, mr.at[there_h * 4 + there_dx], core)
        copy.start()
        noted.append(copy)

    def note_twin(h, dx):
        meta_copy(h, dx, twin, mds, mdr, core).start()

    def noted_here(h, dx):
        meta_copy(h, dx, twin, ms, mr.at[h * 4 + dx], core).wait_recv()
        note_twin(h, dx)

    def all_of(ref, count, send_sem, recv_sem):
        some = ref.at[pl.ds(0, count)]
        return pltpu.make_async_remote_copy(
            src_ref=some, dst_ref=some, send_sem=send_sem, recv_sem=recv_sem, device_id=twin, device_id_type=MESH
        )

    def prepare():
        all_of(meta, 8, mds, mdr).wait_recv()
        named = jnp.concatenate([meta[2 * n] + meta[2 * n + 1] for n in range(NE // 2)], axis=1)
        is_mine = (named[0:4] == e.astype(F32)).astype(F32)
        took = jnp.sum(is_mine, axis=0, keepdims=True)
        its_gate = jnp.sum(is_mine * named[4:8], axis=0, keepdims=True)
        groups = [slice(256 * g, 256 * g + 256) for g in range(NX)]
        by_group = jnp.concatenate([took[:, here] for here in groups] + [jnp.zeros((4, 256), F32)], axis=0)
        position = jnp.dot(by_group.astype(BF16), before[...], preferred_element_type=F32)
        lane, line = (lax.broadcasted_iota(jnp.int32, (8, 256), d) for d in (1, 0))
        first_slot = lane // 128 * 128 + line // 2 * 64 + lane // TOK % 2 * CAP
        slot = jnp.where(by_group > 0.5, position.astype(jnp.int32) + first_slot, -1)
        slot_row = lax.broadcasted_iota(jnp.int32, (256, 256), 0)
        picked = [(slot_row == slot[g : g + 1]).astype(F32).astype(BF16) for g in range(NX)]
        of_tokens = [
            jnp.dot(hid[:, 256 * (g % 2) : 256 * (g % 2) + 256], picked[g], preferred_element_type=F32)
            for g in range(NX)
        ]
        mine[...] = jnp.concatenate([is_mine, jnp.zeros((4, NE * TOK), F32)], axis=0)
        gate[...] = jnp.broadcast_to(its_gate, (8, NE * TOK))
        for g, here in enumerate(groups):
            pick[g] = picked[g]
            hs[:, here] = of_tokens[g].astype(BF16)
            spread[:, here] = (of_tokens[g] * its_gate[:, here]).astype(BF16)

    k0, k1, k2, k3 = cls, (cls + 1) % 4, (cls + 2) % 4, (cls + 3) % 4
    along = ((x1, 3), (x3, 1), (x2, 2))

    load_tok.wait()
    for to, dx in along:
        note(0, 0, to, 0, dx)
        send(0, 0, k0, to, 0, dx)
    crossing = [meta_copy(0, 0, mirror, ms, mr.at[4], core)]
    noted.append(crossing[0])
    crossing += [outgoing(0, 0, k2, mirror, 1, 0, n, first=True) for n in range(STRIPS)]

    @pl.when(half == 0)
    def _():
        pl.semaphore_wait(ready, 1)

    for copy in crossing:
        copy.start()
    note_twin(0, 0)
    share(0, 0, 0, 4)
    send(0, 0, k2, x1, 0, 3)
    send(0, 0, k2, x3, 0, 1)

    t_from = lax.broadcasted_iota(jnp.int32, (256, 256), 0)
    t_to = lax.broadcasted_iota(jnp.int32, (256, 256), 1)
    before[...] = ((t_from < t_to) & (t_from // TOK == t_to // TOK)).astype(F32).astype(BF16)

    arrival(0, 2, k0).wait_recv()
    for to in (y1, y7, zn):
        send(0, 2, k0, to, 0, 2)
    share(0, 2, k0)
    for dx in (1, 3, 2):
        noted_here(0, dx)
    pl.semaphore_wait(wave.at[0], 2)
    ripple(1, y1, y7)

    noted_here(1, 0)
    for to, dx in along:
        note(1, 0, to, 1, dx)
    for n in range(STRIPS):
        arrival(1, 0, k0, n).wait_recv()
        for to, dx in along:
            send(1, 0, k0, to, 1, dx, n, first=True)
        for to in (y1, y7, zn):
            send(1, 0, k0, to, 1, 0, n)
    for kk in (k1, k3):
        send(0, 0, kk, x1, 0, 3)
        send(0, 0, kk, x3, 0, 1)
    share(1, 0, k0)
    for dx in (1, 3, 2):
        noted_here(1, dx)
    pl.semaphore_wait(wave.at[1], 2)
    ripple(2, y1, y7)
    for dx in (1, 3):
        arrival(0, dx, k0).wait_recv()
        share(0, dx, k0)
    for n in range(STRIPS):
        for dx in (1, 3, 2):
            arrival(1, dx, k0, n).wait_recv()
            for to in (y1, y7, zn):
                send(1, dx, k0, to, 1, dx, n)
    for dx in (1, 3, 2):
        share(1, dx, k0)
    pl.semaphore_wait(wave.at[2], 2)
    ripple(3, zn)

    load_h.wait()
    prepare()
    load_w.wait()

    def bring(h, dx):
        for k in (k2, k1, k3):
            arrival(h, dx, k).wait_recv()
            share(h, dx, k)

    by_row = (((1,), (1,)), ((), ()))

    def multiply(i):
        hh = half if i == 0 else 1 - half
        for dx in range(NX):
            if (i, dx) != (0, 0):
                from_twin(i, dx)
        here = pl.ds(pl.multiple_of(hh * 512, 512), 512)
        proj = lax.dot_general(w[...], rows[here, :], by_row, preferred_element_type=F32)
        terms = mine[:, here] * jnp.sum(hs[:, here].astype(F32) * proj, axis=0, keepdims=True)
        for n in range(NX):
            part[i, n] = terms[:, 128 * n : 128 * n + 128]
        for dx in (2, 1, 3, 0):
            xx = (x + dx) % NX
            for cc in range(2):
                if (i, dx, cc) == (0, 0, 0):
                    continue
                pltpu.make_async_remote_copy(
                    src_ref=part.at[i, xx], dst_ref=sc1.at[e], send_sem=s1_s, recv_sem=s1_r,
                    device_id=(expert(xx, hh, core if cc == 0 else 1 - core), y, r if i == 0 else NR - 1 - r),
                    device_id_type=MESH,
                ).start()
        if i == 0:
            sc1[e] = part[0, x]
        scaled[:, here] = (proj * gate[0:1, here]).astype(BF16)

    for dx in (2, 1, 3):
        bring(0, dx)
    bring(1, 0)
    pl.semaphore_wait(wave.at[3], 1)
    ripple(4, far)
    from_twin(0, 0)

    @pl.when(core == 0)
    def _():
        multiply(0)

    for dx in (1, 3, 2):
        bring(1, dx)

    @pl.when(core == 1)
    def _():
        multiply(0)

    multiply(1)

    for n in range(2):
        slots = slice(256 * n, 256 * n + 256)
        gh[:, slots] = sum(
            lax.dot_general(scaled[:, 256 * g : 256 * g + 256], pick[g], by_row, preferred_element_type=F32)
            for g in (n, n + 2)
        ).astype(BF16)

    out_h = pltpu.make_async_copy(gh, gh_hbm, out_sem.at[0])
    out_h.start()

    width = 512

    def weight_columns(first, last):
        for j in range(first, last):
            cols = pl.ds(j * width, width)
            gd[:, cols] = jnp.dot(spread[...], rows[:, cols], preferred_element_type=F32).astype(BF16)

    weight_columns(0, 3)

    all_of(sc1, NE - 1, s1_s, s1_r).wait_recv()
    sc2[plane] = jnp.sum(sc1[...], axis=0)

    def tell(n, _):
        p = (plane + PLANE // 2 + (n + 1) // 2 * (1 - 2 * (n % 2))) % PLANE
        pltpu.make_async_remote_copy(
            src_ref=sc2.at[plane], dst_ref=sc2.at[plane], send_sem=s2_s, recv_sem=s2_r,
            device_id=(e, p // NR, p % NR), device_id_type=MESH,
        ).start()
        return 0

    pl.semaphore_wait(wave.at[4], 1)
    lax.fori_loop(0, PLANE - 1, tell, 0)

    weight_columns(3, gd.shape[1] // width)
    out_d = pltpu.make_async_copy(gd, gd_hbm, out_sem.at[1])
    out_d.start()

    assert len(noted) == 7
    all_of(rows, int(sum(sent)), ss, ss).wait_send()
    all_of(rows, sum(shared), ds, ds).wait_send()
    all_of(meta, len(noted), ms, ms).wait_send()
    all_of(meta, 8, mds, mds).wait_send()
    all_of(sc1, NE - 1, s1_s, s1_s).wait_send()
    out_h.wait()
    out_d.wait()
    exchange = all_of(sc2, PLANE - 1, s2_s, s2_r)
    exchange.wait_recv()
    total = jnp.sum(sc2[...], axis=0)
    scores[...] = jnp.where(core == 0, total[0:TOP, 0:TOK], total[0:TOP, TOK : 2 * TOK])
    out_s = pltpu.make_async_copy(scores, score_hbm, out_sem.at[2])
    out_s.start()
    exchange.wait_send()
    out_s.wait()


def shards(grad_out, gate_probs, expert_ids, saved_hidden, down_weight):
    hidden, weight = saved_hidden[0], down_weight[0]
    units, slots = hidden.shape
    width = weight.shape[1]
    dma = pltpu.SemaphoreType.DMA
    anywhere = pl.BlockSpec(memory_space=pl.ANY)
    hbm = pl.BlockSpec(memory_space=pltpu.HBM)
    gh, gd, scores = pl.pallas_call(
        kernel,
        out_shape=(
            jax.ShapeDtypeStruct((units, slots), BF16),
            jax.ShapeDtypeStruct((units, width), BF16),
            jax.ShapeDtypeStruct((TOP, TOK), F32),
        ),
        in_specs=[hbm] * 5,
        out_specs=(anywhere,) * 3,
        scratch_shapes=[
            pltpu.VMEM((TOP, TOK), F32),
            pltpu.VMEM((TOP, TOK), jnp.int32),
            pltpu.VMEM((TOP, TOK), BF16),
            pltpu.VMEM((NE * TOK, width), BF16),
            pltpu.VMEM((units, width), BF16),
            pltpu.VMEM((units, slots), BF16),
            pltpu.VMEM((units, NE * TOK), BF16),
            pltpu.VMEM((units, NE * TOK), BF16),
            pltpu.VMEM((units, NE * TOK), BF16),
            pltpu.VMEM((NX, 256, 256), BF16),
            pltpu.VMEM((8, NE * TOK), F32),
            pltpu.VMEM((8, NE * TOK), F32),
            pltpu.VMEM((units, slots), BF16),
            pltpu.VMEM((units, width), BF16),
            pltpu.VMEM((256, 256), BF16),
            pltpu.VMEM((NE, 8, 128), F32),
            pltpu.VMEM((2, NX, 8, 128), F32),
            pltpu.VMEM((NE, 8, 128), F32),
            pltpu.VMEM((PLANE, 8, 128), F32),
            dma((5,)),
            dma((3,)),
            dma,
            dma((8, 4)),
            dma((NX, STRIPS)),
            dma,
            dma((8,)),
            dma,
            dma((8,)),
            dma,
            dma,
            dma,
            dma,
            dma,
            dma,
            pltpu.SemaphoreType.REGULAR((5,)),
            pltpu.SemaphoreType.REGULAR,
        ],
        compiler_params=pltpu.CompilerParams(collective_id=0, has_side_effects=True, vmem_limit_bytes=40 * 2**20),
        cost_estimate=pl.CostEstimate(
            flops=4 * units * width * NE * TOK, bytes_accessed=4 * units * width, transcendentals=0
        ),
    )(*(pltpu.with_memory_space_constraint(a, pltpu.HBM) for a in (expert_ids.T, gate_probs.T, grad_out, hidden, weight)))
    return gh[None], gd[None], scores.T


def solution(mesh):
    split = P("expert", ("shard", "replica"), None)
    rows = P("expert", None)
    return jax.shard_map(
        shards, mesh=mesh, in_specs=(rows, rows, rows, split, split), out_specs=(split, split, rows), check_vma=False
    )
```

```python
import functools

import jax
import jax.numpy as jnp
from jax import lax
from jax.experimental import pallas as pl
from jax.experimental.pallas import tpu as pltpu
from jax.sharding import PartitionSpec as P

MESH = pl.DeviceIdType.MESH
NX, NY, NR = 4, 8, 4
NE = 16
TOK, TOP, CAP = 64, 4, 32
CH = 16
STRIPS = 2
PLANE = NY * NR
F32, BF16 = jnp.float32, jnp.bfloat16


def kernel(
    ids_hbm, gates_hbm, tok_hbm, hid_hbm, w_hbm,
    gh_hbm, gd_hbm, score_hbm,
    scores, ids, gates, rows, w, hid, spread, hs, scaled, pick, mine, gate, gh, gd, before, meta, part, sc1, sc2,
    load_sem, out_sem, ss, rs, rb, ds, rd, ms, mr, mds, mdr, s1_s, s1_r, s2_s, s2_r, wave, ready,
):
    e, y, r = lax.axis_index("expert"), lax.axis_index("shard"), lax.axis_index("replica")
    x, half, core = e // 4, (e // 2) % 2, e % 2
    plane = y * NR + r
    cls = (y + 2 * r) % 4

    def expert(xx, hh, cc):
        return xx * 4 + hh * 2 + cc

    def block(xx, hh, cc):
        return hh * 8 + xx * 2 + cc

    own = block(x, half, core)
    x1 = (expert((x + 1) % NX, half, core), y, r)
    x3 = (expert((x + 3) % NX, half, core), y, r)
    x2 = (expert((x + 2) % NX, half, core), y, r)
    y1, y7 = (e, (y + 1) % NY, r), (e, (y + 7) % NY, r)
    zn = (e, y, r + 1 - 2 * (r % 2))
    far = (e, y, (r + 2) % NR)
    mirror = (expert(x, 1 - half, core), y, NR - 1 - r)
    twin = (expert(x, half, 1 - core), y, r)

    barrier = pltpu.get_barrier_semaphore()
    near = (x1, x3, x2, y1, y7, zn, far, twin)
    for other in near:
        pl.semaphore_signal(barrier, inc=1, device_id=other, device_id_type=MESH)

    @pl.when(half == 0)
    def _():
        pl.semaphore_signal(barrier, inc=1, device_id=mirror, device_id_type=MESH)

    own_row = pl.multiple_of(own * TOK, TOK)
    load_tok = pltpu.make_async_copy(tok_hbm, rows.at[pl.ds(own_row, TOK)], load_sem.at[0])
    load_w = pltpu.make_async_copy(w_hbm, w, load_sem.at[1])
    load_h = pltpu.make_async_copy(hid_hbm, hid, load_sem.at[2])
    load_ids = pltpu.make_async_copy(ids_hbm, ids, load_sem.at[3])
    load_gates = pltpu.make_async_copy(gates_hbm, gates, load_sem.at[4])
    load_tok.start()
    load_ids.start()
    load_gates.start()
    load_w.start()
    load_h.start()

    place = (
        lax.broadcasted_iota(jnp.int32, (TOK, 128), 1)
        == lax.broadcasted_iota(jnp.int32, (TOK, 128), 0) + TOK * core
    ).astype(F32).astype(BF16)
    load_ids.wait()
    load_gates.wait()
    meta[own, 0:4, :] = jnp.dot(ids[...].astype(F32).astype(BF16), place, preferred_element_type=F32)
    meta[own, 4:8, :] = jnp.dot(gates[...], place, preferred_element_type=F32)
    pl.semaphore_wait(barrier, len(near) + half)

    @pl.when(half == 1)
    def _():
        pl.semaphore_signal(ready, inc=1, device_id=mirror, device_id_type=MESH)

    def ripple(n, *others):
        for other in others:
            pl.semaphore_signal(wave.at[n], inc=1, device_id=other, device_id_type=MESH)

    ripple(0, y1, y7)

    sent, shared = [], []

    def block_row(h, dx, cc, k):
        b = block((x + dx) % NX, half if h == 0 else 1 - half, cc)
        return pl.multiple_of(b * TOK + k * CH, CH)

    wide = rows.shape[1]
    whole = pl.ds(0, wide)
    strips = [pl.ds(n * (wide // STRIPS), wide // STRIPS) for n in range(STRIPS)]

    def arrival(h, dx, k, n=None):
        ref = rows.at[pl.ds(block_row(h, dx, core, k), CH), whole if n is None else strips[n]]
        sem = rs.at[h * 4 + dx, k] if n is None else rb.at[dx, n]
        return pltpu.make_async_remote_copy(
            src_ref=ref, dst_ref=ref, send_sem=ss, recv_sem=sem, device_id=x1, device_id_type=MESH
        )

    def from_twin(h, dx):
        ref = rows.at[pl.ds(block_row(h, dx, 1 - core, 0), TOK)]
        pltpu.make_async_remote_copy(
            src_ref=ref, dst_ref=ref, send_sem=ss, recv_sem=rd.at[h * 4 + dx], device_id=twin, device_id_type=MESH
        ).wait_recv()

    def outgoing(h, dx, k, to, there_h, there_dx, n=None, first=False):
        ref = rows.at[pl.ds(block_row(h, dx, core, k), CH), whole if n is None else strips[n]]
        sem = rb.at[there_dx, n] if first else rs.at[there_h * 4 + there_dx, k]
        copy = pltpu.make_async_remote_copy(
            src_ref=ref, dst_ref=ref, send_sem=ss, recv_sem=sem, device_id=to, device_id_type=MESH
        )
        sent.append(CH if n is None else CH / STRIPS)
        return copy

    def send(*what, **how):
        outgoing(*what, **how).start()

    def share(h, dx, k, count=1):
        ref = rows.at[pl.ds(block_row(h, dx, core, k), CH * count)]
        copy = pltpu.make_async_remote_copy(
            src_ref=ref, dst_ref=ref, send_sem=ds, recv_sem=rd.at[h * 4 + dx],
            device_id=twin, device_id_type=MESH,
        )
        copy.start()
        shared.append(CH * count)

    def meta_copy(h, dx, to, send_sem, recv_sem, cc):
        ref = meta.at[block((x + dx) % NX, half if h == 0 else 1 - half, cc)]
        return pltpu.make_async_remote_copy(
            src_ref=ref, dst_ref=ref, send_sem=send_sem, recv_sem=recv_sem, device_id=to, device_id_type=MESH
        )

    noted = []

    def note(h, dx, to, there_h, there_dx):
        copy = meta_copy(h, dx, to, ms, mr.at[there_h * 4 + there_dx], core)
        copy.start()
        noted.append(copy)

    def note_twin(h, dx):
        meta_copy(h, dx, twin, mds, mdr, core).start()

    def noted_here(h, dx):
        meta_copy(h, dx, twin, ms, mr.at[h * 4 + dx], core).wait_recv()
        note_twin(h, dx)

    def all_of(ref, count, send_sem, recv_sem):
        some = ref.at[pl.ds(0, count)]
        return pltpu.make_async_remote_copy(
            src_ref=some, dst_ref=some, send_sem=send_sem, recv_sem=recv_sem, device_id=twin, device_id_type=MESH
        )

    def prepare():
        all_of(meta, 8, mds, mdr).wait_recv()
        named = jnp.concatenate([meta[2 * n] + meta[2 * n + 1] for n in range(NE // 2)], axis=1)
        is_mine = (named[0:4] == e.astype(F32)).astype(F32)
        took = jnp.sum(is_mine, axis=0, keepdims=True)
        its_gate = jnp.sum(is_mine * named[4:8], axis=0, keepdims=True)
        groups = [slice(256 * g, 256 * g + 256) for g in range(NX)]
        by_group = jnp.concatenate([took[:, here] for here in groups] + [jnp.zeros((4, 256), F32)], axis=0)
        position = jnp.dot(by_group.astype(BF16), before[...], preferred_element_type=F32)
        lane, line = (lax.broadcasted_iota(jnp.int32, (8, 256), d) for d in (1, 0))
        first_slot = lane // 128 * 128 + line // 2 * 64 + lane // TOK % 2 * CAP
        slot = jnp.where(by_group > 0.5, position.astype(jnp.int32) + first_slot, -1)
        slot_row = lax.broadcasted_iota(jnp.int32, (256, 256), 0)
        picked = [(slot_row == slot[g : g + 1]).astype(F32).astype(BF16) for g in range(NX)]
        of_tokens = [
            jnp.dot(hid[:, 256 * (g % 2) : 256 * (g % 2) + 256], picked[g], preferred_element_type=F32)
            for g in range(NX)
        ]
        mine[...] = jnp.concatenate([is_mine, jnp.zeros((4, NE * TOK), F32)], axis=0)
        gate[...] = jnp.broadcast_to(its_gate, (8, NE * TOK))
        for g, here in enumerate(groups):
            pick[g] = picked[g]
            hs[:, here] = of_tokens[g].astype(BF16)
            spread[:, here] = (of_tokens[g] * its_gate[:, here]).astype(BF16)

    k0, k1, k2, k3 = cls, (cls + 1) % 4, (cls + 2) % 4, (cls + 3) % 4
    along = ((x1, 3), (x3, 1), (x2, 2))

    load_tok.wait()
    crossing = [meta_copy(0, 0, mirror, ms, mr.at[4], core)]
    noted.append(crossing[0])
    crossing += [outgoing(0, 0, k2, mirror, 1, 0, n, first=True) for n in range(STRIPS)]

    @pl.when(half == 1)
    def _():
        for copy in crossing:
            copy.start()

    for to, dx in along:
        note(0, 0, to, 0, dx)
        send(0, 0, k0, to, 0, dx)

    @pl.when(half == 0)
    def _():
        pl.semaphore_wait(ready, 1)
        for copy in crossing:
            copy.start()

    note_twin(0, 0)
    share(0, 0, 0, 4)
    send(0, 0, k2, x1, 0, 3)
    send(0, 0, k2, x3, 0, 1)

    t_from = lax.broadcasted_iota(jnp.int32, (256, 256), 0)
    t_to = lax.broadcasted_iota(jnp.int32, (256, 256), 1)
    before[...] = ((t_from < t_to) & (t_from // TOK == t_to // TOK)).astype(F32).astype(BF16)

    arrival(0, 2, k0).wait_recv()
    for to in (y1, y7, zn):
        send(0, 2, k0, to, 0, 2)
    share(0, 2, k0)
    for dx in (1, 3, 2):
        noted_here(0, dx)
    pl.semaphore_wait(wave.at[0], 2)
    ripple(1, y1, y7)

    noted_here(1, 0)
    for to, dx in along:
        note(1, 0, to, 1, dx)
    for n in range(STRIPS):
        arrival(1, 0, k0, n).wait_recv()
        for to, dx in along:
            send(1, 0, k0, to, 1, dx, n, first=True)
        for to in (y1, y7, zn):
            send(1, 0, k0, to, 1, 0, n)
    for kk in (k1, k3):
        send(0, 0, kk, x1, 0, 3)
        send(0, 0, kk, x3, 0, 1)
    share(1, 0, k0)
    for dx in (1, 3, 2):
        noted_here(1, dx)
    pl.semaphore_wait(wave.at[1], 2)
    ripple(2, y1, y7)
    for dx in (1, 3):
        arrival(0, dx, k0).wait_recv()
        share(0, dx, k0)
    for n in range(STRIPS):
        for dx in (1, 3, 2):
            arrival(1, dx, k0, n).wait_recv()
            for to in (y1, y7, zn):
                send(1, dx, k0, to, 1, dx, n)
    for dx in (1, 3, 2):
        share(1, dx, k0)
    pl.semaphore_wait(wave.at[2], 2)
    ripple(3, zn)

    load_h.wait()
    prepare()
    load_w.wait()

    def bring(h, dx):
        for k in (k2, k1, k3):
            arrival(h, dx, k).wait_recv()
            share(h, dx, k)

    by_row = (((1,), (1,)), ((), ()))

    def multiply(i):
        hh = half if i == 0 else 1 - half
        for dx in range(NX):
            if (i, dx) != (0, 0):
                from_twin(i, dx)
        here = pl.ds(pl.multiple_of(hh * 512, 512), 512)
        proj = lax.dot_general(w[...], rows[here, :], by_row, preferred_element_type=F32)
        terms = mine[:, here] * jnp.sum(hs[:, here].astype(F32) * proj, axis=0, keepdims=True)
        for n in range(NX):
            part[i, n] = terms[:, 128 * n : 128 * n + 128]
        for dx in (2, 1, 3, 0):
            xx = (x + dx) % NX
            for cc in range(2):
                if (i, dx, cc) == (0, 0, 0):
                    continue
                pltpu.make_async_remote_copy(
                    src_ref=part.at[i, xx], dst_ref=sc1.at[e], send_sem=s1_s, recv_sem=s1_r,
                    device_id=(expert(xx, hh, core if cc == 0 else 1 - core), y, r if i == 0 else NR - 1 - r),
                    device_id_type=MESH,
                ).start()
        if i == 0:
            sc1[e] = part[0, x]
        scaled[:, here] = (proj * gate[0:1, here]).astype(BF16)

    for dx in (2, 1, 3):
        bring(0, dx)
    bring(1, 0)
    pl.semaphore_wait(wave.at[3], 1)
    ripple(4, far)
    from_twin(0, 0)

    @pl.when(core == 0)
    def _():
        multiply(0)

    for dx in (1, 3, 2):
        bring(1, dx)

    @pl.when(core == 1)
    def _():
        multiply(0)

    multiply(1)

    for n in range(2):
        slots = slice(256 * n, 256 * n + 256)
        gh[:, slots] = sum(
            lax.dot_general(scaled[:, 256 * g : 256 * g + 256], pick[g], by_row, preferred_element_type=F32)
            for g in (n, n + 2)
        ).astype(BF16)

    out_h = pltpu.make_async_copy(gh, gh_hbm, out_sem.at[0])
    out_h.start()

    width = 512

    def weight_columns(first, last):
        for j in range(first, last):
            cols = pl.ds(j * width, width)
            gd[:, cols] = jnp.dot(spread[...], rows[:, cols], preferred_element_type=F32).astype(BF16)

    weight_columns(0, 3)

    all_of(sc1, NE - 1, s1_s, s1_r).wait_recv()
    sc2[plane] = jnp.sum(sc1[...], axis=0)

    def tell(n, _):
        p = (plane + PLANE // 2 + (n + 1) // 2 * (1 - 2 * (n % 2))) % PLANE
        pltpu.make_async_remote_copy(
            src_ref=sc2.at[plane], dst_ref=sc2.at[plane], send_sem=s2_s, recv_sem=s2_r,
            device_id=(e, p // NR, p % NR), device_id_type=MESH,
        ).start()
        return 0

    pl.semaphore_wait(wave.at[4], 1)
    lax.fori_loop(0, PLANE - 1, tell, 0)

    weight_columns(3, gd.shape[1] // width)
    out_d = pltpu.make_async_copy(gd, gd_hbm, out_sem.at[1])
    out_d.start()

    assert len(noted) == 7
    all_of(rows, int(sum(sent)), ss, ss).wait_send()
    all_of(rows, sum(shared), ds, ds).wait_send()
    all_of(meta, len(noted), ms, ms).wait_send()
    all_of(meta, 8, mds, mds).wait_send()
    all_of(sc1, NE - 1, s1_s, s1_s).wait_send()
    out_h.wait()
    out_d.wait()
    exchange = all_of(sc2, PLANE - 1, s2_s, s2_r)
    exchange.wait_recv()
    total = jnp.sum(sc2[...], axis=0)
    scores[...] = jnp.where(core == 0, total[0:TOP, 0:TOK], total[0:TOP, TOK : 2 * TOK])
    out_s = pltpu.make_async_copy(scores, score_hbm, out_sem.at[2])
    out_s.start()
    exchange.wait_send()
    out_s.wait()


def shards(grad_out, gate_probs, expert_ids, saved_hidden, down_weight):
    hidden, weight = saved_hidden[0], down_weight[0]
    units, slots = hidden.shape
    width = weight.shape[1]
    dma = pltpu.SemaphoreType.DMA
    anywhere = pl.BlockSpec(memory_space=pl.ANY)
    hbm = pl.BlockSpec(memory_space=pltpu.HBM)
    gh, gd, scores = pl.pallas_call(
        kernel,
        out_shape=(
            jax.ShapeDtypeStruct((units, slots), BF16),
            jax.ShapeDtypeStruct((units, width), BF16),
            jax.ShapeDtypeStruct((TOP, TOK), F32),
        ),
        in_specs=[hbm] * 5,
        out_specs=(anywhere,) * 3,
        scratch_shapes=[
            pltpu.VMEM((TOP, TOK), F32),
            pltpu.VMEM((TOP, TOK), jnp.int32),
            pltpu.VMEM((TOP, TOK), BF16),
            pltpu.VMEM((NE * TOK, width), BF16),
            pltpu.VMEM((units, width), BF16),
            pltpu.VMEM((units, slots), BF16),
            pltpu.VMEM((units, NE * TOK), BF16),
            pltpu.VMEM((units, NE * TOK), BF16),
            pltpu.VMEM((units, NE * TOK), BF16),
            pltpu.VMEM((NX, 256, 256), BF16),
            pltpu.VMEM((8, NE * TOK), F32),
            pltpu.VMEM((8, NE * TOK), F32),
            pltpu.VMEM((units, slots), BF16),
            pltpu.VMEM((units, width), BF16),
            pltpu.VMEM((256, 256), BF16),
            pltpu.VMEM((NE, 8, 128), F32),
            pltpu.VMEM((2, NX, 8, 128), F32),
            pltpu.VMEM((NE, 8, 128), F32),
            pltpu.VMEM((PLANE, 8, 128), F32),
            dma((5,)),
            dma((3,)),
            dma,
            dma((8, 4)),
            dma((NX, STRIPS)),
            dma,
            dma((8,)),
            dma,
            dma((8,)),
            dma,
            dma,
            dma,
            dma,
            dma,
            dma,
            pltpu.SemaphoreType.REGULAR((5,)),
            pltpu.SemaphoreType.REGULAR,
        ],
        compiler_params=pltpu.CompilerParams(collective_id=0, has_side_effects=True, vmem_limit_bytes=40 * 2**20),
        cost_estimate=pl.CostEstimate(
            flops=4 * units * width * NE * TOK, bytes_accessed=4 * units * width, transcendentals=0
        ),
    )(*(pltpu.with_memory_space_constraint(a, pltpu.HBM) for a in (expert_ids.T, gate_probs.T, grad_out, hidden, weight)))
    return gh[None], gd[None], scores.T


def solution(mesh):
    split = P("expert", ("shard", "replica"), None)
    rows = P("expert", None)
    return jax.shard_map(
        shards, mesh=mesh, in_specs=(rows, rows, rows, split, split), out_specs=(split, split, rows), check_vma=False
    )
```
